32 devices in a mesh: crop: 2 (over y), row: 4 (over z), col: 2 (over x), chan: 2 (over core).
Axes of the slice: x: 2, y: 2, z: 4, core: 2. Of those that a mesh axis runs over, the one named last changes fastest.
Arguments:
- pair_act: bfloat16 [256, 128, 128], P(('crop', 'row'), 'col'), parts along dimension 0, may hold values from -10 to 10
- input_gain: float32 [128], replicated, may hold values from 0.1 to 1.9
- left_proj: bfloat16 [128, 128], replicated, may hold values from -0.5 to 0.5
- left_gate: bfloat16 [128, 128], replicated, may hold values from -0.5 to 0.5
- right_proj: bfloat16 [128, 128], replicated, may hold values from -0.5 to 0.5
- right_gate: bfloat16 [128, 128], replicated, may hold values from -0.5 to 0.5
- output_gain: float32 [128], replicated, may hold values from 0.1 to 1.9
- out_gate: bfloat16 [128, 128], replicated, may hold values from -0.5 to 0.5
- out_proj: bfloat16 [128, 128], replicated, may hold values from -0.5 to 0.5
Outputs:
- update: bfloat16 [256, 128, 128], P(('crop', 'row'), 'col', 'chan'), parts along dimension 0
The draws below stay inside these ranges and needn't reach their ends.
There are 2 independent parts, one for each index of `crop`. The reference program is written for one: setup_inputs(seed, part) draws one part's arguments, and reference() takes and returns one part's arrays. A program takes and returns all parts, laid end to end along the dimension named above; an argument that names none is the same for every part. Nothing has to cross between parts.
All inputs are finite; a program needn't handle non-finite values.
Results may differ from the reference program's by a relative error of at most 0.012.
Values may be sent and summed in bfloat16 or wider, within the bound.
A program may use at most 64 MiB of HBM per device.

```python
import math
import jax
import jax.numpy as jnp
from jax import lax

C = 128
HID = 128
N = 128


def draw_pair_act(key, part):
    key = jax.random.fold_in(key, 11)
    key_values, key_scale, key_shift = jax.random.split(key, 3)
    values = jnp.clip(jax.random.normal(key_values, (N, N, C), jnp.float32), -3.0, 3.0)
    scale = jnp.exp(jax.random.uniform(key_scale, (N, N, 1), jnp.float32, math.log(0.3), math.log(3.0)))
    shift = jax.random.uniform(key_shift, (N, N, 1), jnp.float32, -1.0, 1.0)
    return (shift + scale * values).astype(jnp.bfloat16)


def normal_values(stream_key, shape, deviation, reach, held_as=jnp.bfloat16):
    return jnp.clip(deviation * jax.random.normal(stream_key, shape, jnp.float32), -reach, reach).astype(held_as)


def setup_inputs(seed: int = 0, part: int = 0) -> dict:
    keys = jax.random.split(jax.random.key(seed), 10)
    own_keys = jax.random.split(jax.random.fold_in(keys[9], part), 10)
    return {
        "pair_act": draw_pair_act(jax.random.fold_in(jax.random.fold_in(keys[9], part), 71), part),
        "input_gain": jnp.clip(1.0 + 0.18 * jax.random.normal(keys[1], (C,), jnp.float32), 0.1, 1.9),
        "left_proj": normal_values(keys[2], (C, HID), C ** -0.5, 0.5),
        "left_gate": normal_values(keys[3], (C, HID), C ** -0.5, 0.5),
        "right_proj": normal_values(keys[4], (C, HID), C ** -0.5, 0.5),
        "right_gate": normal_values(keys[5], (C, HID), C ** -0.5, 0.5),
        "output_gain": jnp.clip(1.0 + 0.18 * jax.random.normal(keys[6], (HID,), jnp.float32), 0.1, 1.9),
        "out_gate": normal_values(keys[7], (C, C), C ** -0.5, 0.5),
        "out_proj": normal_values(keys[8], (HID, C), HID ** -0.5, 0.5),
    }


epsilon = 1e-05

def normalize(values, scaling):
    average = lax.optimization_barrier(jnp.mean(values, axis=-1, keepdims=True))
    variance = lax.optimization_barrier(jnp.mean(values * values, axis=-1, keepdims=True)) - average * average
    return (values - average) * lax.rsqrt(variance + epsilon) * scaling

def project(normed, weights):
    flattened = normed.reshape(-1, normed.shape[-1])
    result = jnp.dot(flattened, weights, preferred_element_type=jnp.float32)
    return result.reshape(normed.shape[:-1] + (weights.shape[1],))

def reference(pair_act, input_gain, left_proj, left_gate, right_proj, right_gate, output_gain, out_gate, out_proj):
    normed = normalize(pair_act.astype(jnp.float32), input_gain).astype(jnp.bfloat16)
    left_act = (jax.nn.sigmoid(project(normed, left_gate)) * project(normed, left_proj)).astype(jnp.bfloat16)
    right_act = (jax.nn.sigmoid(project(normed, right_gate)) * project(normed, right_proj)).astype(jnp.bfloat16)
    triangle = jnp.einsum('ikc,jkc->ijc', left_act.astype(jnp.float32), right_act.astype(jnp.float32)).astype(jnp.bfloat16)
    tri_norm = normalize(triangle.astype(jnp.float32), output_gain).astype(jnp.bfloat16)
    gating = jax.nn.sigmoid(project(normed, out_gate))
    return (gating * project(tri_norm, out_proj)).astype(jnp.bfloat16)
```

```python
import functools

import jax
import jax.numpy as jnp
from jax import lax
from jax.experimental import pallas as pl
from jax.experimental.pallas import tpu as pltpu
from jax.sharding import PartitionSpec as P

epsilon = 1e-05
MESH = pl.DeviceIdType.MESH
F32 = jnp.float32
BF16 = jnp.bfloat16
CHUNKS = 4
STEP_GROUPS = 4


def nt_dot(a, b):
    return lax.dot_general(a, b, (((1,), (1,)), ((), ())), preferred_element_type=F32)


def kernel(
    n_row,
    n_col,
    pair_ref,
    in_gain_ref,
    lp_ref,
    lg_ref,
    rp_ref,
    rg_ref,
    out_gain_ref,
    og_ref,
    op_ref,
    out_ref,
    wr,
    wl,
    wo,
    zn,
    flat,
    gate,
    left,
    right,
    keep,
    x_out,
    x_in,
    tri,
    flat_tri,
    z_send,
    z_recv,
    x_send,
    x_recv,
    s_send,
    s_recv,
):
    rows, width, channels = pair_ref.shape
    half = rows // 2
    hidden = lp_ref.shape[1]
    slab = hidden // 2
    pairs = slab // 2
    ratio = n_row // n_col
    per = pairs // CHUNKS
    row = lax.axis_index("row")
    col = lax.axis_index("col")
    chan = lax.axis_index("chan")

    def slot(block):
        return lax.rem(block - ratio * col + n_row, n_row)

    barrier = pltpu.get_barrier_semaphore()

    @pl.when(row + 1 < n_row)
    def _():
        pl.semaphore_signal(barrier, inc=1, device_id={"row": row + 1}, device_id_type=MESH)

    @pl.when(row >= 1)
    def _():
        pl.semaphore_signal(barrier, inc=1, device_id={"row": row - 1}, device_id_type=MESH)

    for d in range(1, n_col):
        pl.semaphore_signal(
            barrier, inc=1, device_id={"col": lax.rem(col + d, n_col)}, device_id_type=MESH
        )
    pl.semaphore_signal(barrier, inc=1, device_id={"chan": 1 - chan}, device_id_type=MESH)

    gain_in = in_gain_ref[...]
    gain_out = out_gain_ref[...]

    def turned(ref, gain):
        w = jnp.transpose(ref[...].astype(F32))
        w = jnp.where(chan == 0, w[:slab], w[slab:])
        return (w * gain).astype(BF16)

    wr[:slab] = turned(rp_ref, gain_in)
    wr[slab:] = turned(rg_ref, gain_in)
    wl[:slab] = turned(lp_ref, gain_in)
    wl[slab : 2 * slab] = turned(lg_ref, gain_in)
    wl[2 * slab :] = turned(og_ref, gain_in)
    wo[...] = turned(op_ref, gain_out)

    low = lax.broadcasted_iota(jnp.int32, (1, 128), 1) < width

    def interleave(a, b):
        first = jnp.where(low, a, pltpu.roll(b, width, 1))
        second = jnp.where(low, pltpu.roll(a, width, 1), b)
        return first, second

    def right_step(t, carry):
        for u in range(STEP_GROUPS):
            g = t * STEP_GROUPS + u
            x = jnp.concatenate([pair_ref[g], pair_ref[g + half]], 0).astype(F32)
            mean = jnp.mean(x, axis=-1, keepdims=True)
            var = jnp.mean(x * x, axis=-1, keepdims=True) - mean * mean
            z = ((x - mean) * lax.rsqrt(var + epsilon)).astype(BF16)
            zn[g] = z
            p = nt_dot(wr[...], z)
            r = jax.nn.sigmoid(p[slab:]) * p[:slab]
            first, second = interleave(r[:pairs], r[pairs:])
            flat[pl.ds(g, pairs, stride=rows), :] = first
            flat[pl.ds(g + half, pairs, stride=rows), :] = second
        return carry

    lax.fori_loop(0, half // STEP_GROUPS, right_step, 0)

    mine = slot(row)

    def z_copy(up, step, q):
        block = row - (step - 1) if up else row + (step - 1)
        there = row + 1 if up else row - 1
        part = right.at[slot(block), pl.ds(q * per, per)]
        lane = 0 if up else 1
        return pltpu.make_async_remote_copy(
            src_ref=part,
            dst_ref=part,
            send_sem=z_send.at[lane, step - 1, q],
            recv_sem=z_recv.at[lane, step - 1, q],
            device_id={"row": there},
            device_id_type=MESH,
        )

    def z_land(up, step, q):
        block = row - step if up else row + step
        part = right.at[slot(block), pl.ds(q * per, per)]
        lane = 0 if up else 1
        return pltpu.make_async_remote_copy(
            src_ref=part,
            dst_ref=part,
            send_sem=z_send.at[lane, step - 1, q],
            recv_sem=z_recv.at[lane, step - 1, q],
            device_id={"row": row},
            device_id_type=MESH,
        )

    def sends(up, step):
        if up:
            return jnp.logical_and(row - (step - 1) >= 0, row + 1 < n_row)
        return jnp.logical_and(row + (step - 1) < n_row, row >= 1)

    def lands(up, step):
        return row - step >= 0 if up else row + step < n_row

    def start_send(step, q):
        for up in (True, False):

            @pl.when(sends(up, step))
            def _():
                z_copy(up, step, q).start()

    def wait_land(step, q):
        for up in (True, False):

            @pl.when(lands(up, step))
            def _():
                z_land(up, step, q).wait_recv()

    middle = jnp.where(row >= 1, 1, 0) + jnp.where(row + 1 < n_row, 1, 0)
    pl.semaphore_wait(barrier, middle + n_col)

    for q in range(CHUNKS):
        span = flat[pl.ds(q * per * rows, per * rows), :].astype(BF16)
        right[mine, pl.ds(q * per, per)] = span.reshape(per, rows, 128)
        start_send(1, q)

    def left_step(t, carry):
        for u in range(STEP_GROUPS):
            g = t * STEP_GROUPS + u
            p = nt_dot(wl[...], zn[g])
            r = jax.nn.sigmoid(p[slab : 2 * slab]) * p[:slab]
            gate[g] = jax.nn.sigmoid(p[2 * slab :])
            first, second = interleave(r[:pairs], r[pairs:])
            flat[pl.ds(g, pairs, stride=rows), :] = first
            flat[pl.ds(g + half, pairs, stride=rows), :] = second
        return carry

    lax.fori_loop(0, half // STEP_GROUPS, left_step, 0)

    def left_mask(t, carry):
        for u in range(per):
            c = t * per + u
            f = flat[pl.ds(pl.multiple_of(c * rows, rows), rows), :]
            first = jnp.where(low, f, 0.0)
            second = jnp.where(low, 0.0, f)
            left[c] = jnp.concatenate(
                [first[:half], second[:half], first[half:], second[half:]], 0
            ).astype(BF16)
        return carry

    for step in range(1, n_row):
        for q in range(CHUNKS):
            if step == 1 and q == 0:
                lax.fori_loop(0, pairs // per, left_mask, 0)
            wait_land(step, q)
            if step + 1 < n_row:
                start_send(step + 1, q)
                continue
            contract(
                q, per, rows, n_row, n_col, col, left, right, keep, x_out, x_in,
                x_send, x_recv, interleave,
            )
            if q >= 1:
                combine(q - 1, per, n_col, col, chan, keep, x_out, x_in, tri, x_send, x_recv, s_send, s_recv)
    combine(CHUNKS - 1, per, n_col, col, chan, keep, x_out, x_in, tri, x_send, x_recv, s_send, s_recv)

    for q in range(CHUNKS):
        s_copy(1 - chan, q, per, chan, tri, s_send, s_recv).wait_recv()

    def stat_step(t, carry):
        total, square = carry
        for u in range(per):
            c = t * per + u
            for h in range(2):
                v = tri[h, c].astype(F32)
                a, b = v[:half], v[half:]
                total = total + (a + b)
                square = square + (a * a + b * b)
        return total, square

    zero = jnp.zeros((half, 128), F32)
    total, square = lax.fori_loop(0, pairs // per, stat_step, (zero, zero))
    mean = total * (1.0 / hidden)
    var = square * (1.0 / hidden) - mean * mean
    scale = lax.rsqrt(var + epsilon)

    def norm_step(t, carry):
        for u in range(per):
            c = t * per + u
            for h in range(2):
                v = tri[h, c].astype(F32)
                for k in range(2):
                    at = pl.multiple_of(((h * 2 + k) * pairs + c) * half, half)
                    flat_tri[pl.ds(at, half), :] = (v[k * half : (k + 1) * half] - mean) * scale
        return carry

    lax.fori_loop(0, pairs // per, norm_step, 0)

    def out_step(t, carry):
        for u in range(STEP_GROUPS):
            g = t * STEP_GROUPS + u
            v = flat_tri[pl.ds(g, hidden, stride=half), :].astype(BF16)
            y = jnp.dot(wo[...], v, preferred_element_type=F32) * gate[g]
            y = jnp.transpose(y).astype(BF16)
            out_ref[g] = y[:width]
            out_ref[g + half] = y[width:]
        return carry

    lax.fori_loop(0, half // STEP_GROUPS, out_step, 0)

    for step in range(1, n_row):
        for q in range(CHUNKS):
            for up in (True, False):

                @pl.when(sends(up, step))
                def _():
                    z_copy(up, step, q).wait_send()

    for q in range(CHUNKS):
        for d in range(1, n_col):
            x_copy(d, q, per, n_col, col, x_out, x_in, x_send, x_recv).wait_send()
        s_copy(chan, q, per, chan, tri, s_send, s_recv).wait_send()


def x_copy(d, q, per, n_col, col, x_out, x_in, x_send, x_recv):
    return pltpu.make_async_remote_copy(
        src_ref=x_out.at[d - 1, pl.ds(q * per, per)],
        dst_ref=x_in.at[d - 1, pl.ds(q * per, per)],
        send_sem=x_send.at[d - 1, q],
        recv_sem=x_recv.at[d - 1, q],
        device_id={"col": lax.rem(col + d, n_col)},
        device_id_type=MESH,
    )


def s_copy(which, q, per, chan, tri, s_send, s_recv):
    part = tri.at[which, pl.ds(q * per, per)]
    return pltpu.make_async_remote_copy(
        src_ref=part,
        dst_ref=part,
        send_sem=s_send.at[q],
        recv_sem=s_recv.at[q],
        device_id={"chan": 1 - chan},
        device_id_type=MESH,
    )


def contract(
    q, per, rows, n_row, n_col, col, left, right, keep, x_out, x_in, x_send, x_recv, interleave
):
    for u in range(per):
        c = q * per + u
        a = left[c]
        for m in range(n_col // 2):
            blocks = n_row // (n_col // 2)
            b = jnp.concatenate([right[m * blocks + s, c] for s in range(blocks)], 0)
            t = nt_dot(a, b)
            even, odd = interleave(t[:rows], t[rows:])
            if m == 0:
                keep[c] = even
            else:
                x_out[2 * m - 1, c] = even.astype(BF16)
            x_out[2 * m, c] = odd.astype(BF16)
    for d in range(1, n_col):
        x_copy(d, q, per, n_col, col, x_out, x_in, x_send, x_recv).start()


def combine(
    q, per, n_col, col, chan, keep, x_out, x_in, tri, x_send, x_recv, s_send, s_recv
):
    for d in range(1, n_col):
        x_copy(d, q, per, n_col, col, x_out, x_in, x_send, x_recv).wait_recv()
    for u in range(per):
        c = q * per + u
        v = keep[c]
        for d in range(1, n_col):
            v = v + x_in[d - 1, c].astype(F32)
        tri[chan, c] = v.astype(BF16)
    s_copy(chan, q, per, chan, tri, s_send, s_recv).start()


def on_device(pair_act, input_gain, lp, lg, rp, rg, output_gain, og, op):
    rows, width, channels = pair_act.shape
    hidden = lp.shape[1]
    slab = hidden // 2
    pairs = slab // 2
    half = rows // 2
    n_row = lax.axis_size("row")
    n_col = lax.axis_size("col")
    vmem = pl.BlockSpec(memory_space=pltpu.VMEM)
    dma = pltpu.SemaphoreType.DMA
    return pl.pallas_call(
        functools.partial(kernel, n_row, n_col),
        out_shape=jax.ShapeDtypeStruct((rows, width, channels // 2), BF16),
        in_specs=[vmem] * 9,
        out_specs=vmem,
        scratch_shapes=[
            pltpu.VMEM((2 * slab, channels), BF16),
            pltpu.VMEM((3 * slab, channels), BF16),
            pltpu.VMEM((channels // 2, hidden), BF16),
            pltpu.VMEM((half, 2 * width, channels), BF16),
            pltpu.VMEM((pairs * rows, 128), F32),
            pltpu.VMEM((half, channels // 2, 128), F32),
            pltpu.VMEM((pairs, 2 * rows, 128), BF16),
            pltpu.VMEM((n_row, pairs, rows, 128), BF16),
            pltpu.VMEM((pairs, rows, 128), F32),
            pltpu.VMEM((n_col - 1, pairs, rows, 128), BF16),
            pltpu.VMEM((n_col - 1, pairs, rows, 128), BF16),
            pltpu.VMEM((2, pairs, rows, 128), BF16),
            pltpu.VMEM((hidden * half, 128), F32),
            dma((2, n_row - 1, CHUNKS)),
            dma((2, n_row - 1, CHUNKS)),
            dma((n_col - 1, CHUNKS)),
            dma((n_col - 1, CHUNKS)),
            dma((CHUNKS,)),
            dma((CHUNKS,)),
        ],
        compiler_params=pltpu.CompilerParams(
            collective_id=0, has_side_effects=True, vmem_limit_bytes=48 * 2**20
        ),
    )(
        pair_act,
        input_gain.reshape(1, channels),
        lp,
        lg,
        rp,
        rg,
        output_gain.reshape(1, hidden),
        og,
        op,
    )


def solution(mesh):
    placed = (P(("crop", "row"), "col", None), P(), P(), P(), P(), P(), P(), P(), P())
    return jax.shard_map(
        on_device,
        mesh=mesh,
        in_specs=placed,
        out_specs=P(("crop", "row"), "col", "chan"),
        check_vma=False,
    )
```

```python
import functools

import jax
import jax.numpy as jnp
from jax import lax
from jax.experimental import pallas as pl
from jax.experimental.pallas import tpu as pltpu
from jax.sharding import PartitionSpec as P

epsilon = 1e-05
MESH = pl.DeviceIdType.MESH
F32 = jnp.float32
BF16 = jnp.bfloat16
CHUNKS = 4
STEP_GROUPS = 4


def nt_dot(a, b):
    return lax.dot_general(a, b, (((1,), (1,)), ((), ())), preferred_element_type=F32)


def kernel(
    n_row,
    n_col,
    pair_hbm,
    in_gain_hbm,
    lp_hbm,
    lg_hbm,
    rp_hbm,
    rg_hbm,
    out_gain_hbm,
    og_hbm,
    op_hbm,
    out_ref,
    pair_ref,
    gains,
    weights,
    in_sem,
    wr,
    wl,
    wo,
    zn,
    flat,
    gate,
    left,
    right,
    keep,
    x_out,
    x_in,
    tri,
    flat_tri,
    z_send,
    z_recv,
    x_send,
    x_recv,
    s_send,
    s_recv,
):
    rows, width, channels = pair_hbm.shape
    half = rows // 2
    hidden = lp_hbm.shape[1]
    slab = hidden // 2
    pairs = slab // 2
    ratio = n_row // n_col
    per = pairs // CHUNKS
    row = lax.axis_index("row")
    col = lax.axis_index("col")
    chan = lax.axis_index("chan")

    def slot(block):
        return lax.rem(block - ratio * col + n_row, n_row)

    fetches = [
        pltpu.make_async_copy(source, target, in_sem.at[index])
        for index, (source, target) in enumerate(
            [
                (rp_hbm, weights.at[0]),
                (rg_hbm, weights.at[1]),
                (in_gain_hbm, gains.at[0]),
                (pair_hbm, pair_ref),
                (lp_hbm, weights.at[2]),
                (lg_hbm, weights.at[3]),
                (og_hbm, weights.at[4]),
                (op_hbm, weights.at[5]),
                (out_gain_hbm, gains.at[1]),
            ]
        )
    ]
    for fetch in fetches:
        fetch.start()

    barrier = pltpu.get_barrier_semaphore()

    @pl.when(row + 1 < n_row)
    def _():
        pl.semaphore_signal(barrier, inc=1, device_id={"row": row + 1}, device_id_type=MESH)

    @pl.when(row >= 1)
    def _():
        pl.semaphore_signal(barrier, inc=1, device_id={"row": row - 1}, device_id_type=MESH)

    for d in range(1, n_col):
        pl.semaphore_signal(
            barrier, inc=1, device_id={"col": lax.rem(col + d, n_col)}, device_id_type=MESH
        )
    pl.semaphore_signal(barrier, inc=1, device_id={"chan": 1 - chan}, device_id_type=MESH)

    def turned(index, gain):
        w = jnp.transpose(weights[index].astype(F32))
        w = jnp.where(chan == 0, w[:slab], w[slab:])
        return (w * gain).astype(BF16)

    for fetch in fetches[:3]:
        fetch.wait()
    gain_in = gains[0]
    wr[:slab] = turned(0, gain_in)
    wr[slab:] = turned(1, gain_in)
    fetches[3].wait()

    low = lax.broadcasted_iota(jnp.int32, (1, 128), 1) < width

    def interleave(a, b):
        first = jnp.where(low, a, pltpu.roll(b, width, 1))
        second = jnp.where(low, pltpu.roll(a, width, 1), b)
        return first, second

    def right_step(t, carry):
        for u in range(STEP_GROUPS):
            g = t * STEP_GROUPS + u
            x = jnp.concatenate([pair_ref[g], pair_ref[g + half]], 0).astype(F32)
            mean = jnp.mean(x, axis=-1, keepdims=True)
            var = jnp.mean(x * x, axis=-1, keepdims=True) - mean * mean
            z = ((x - mean) * lax.rsqrt(var + epsilon)).astype(BF16)
            zn[g] = z
            p = nt_dot(wr[...], z)
            r = jax.nn.sigmoid(p[slab:]) * p[:slab]
            first, second = interleave(r[:pairs], r[pairs:])
            flat[pl.ds(g, pairs, stride=rows), :] = first
            flat[pl.ds(g + half, pairs, stride=rows), :] = second
        return carry

    lax.fori_loop(0, half // STEP_GROUPS, right_step, 0)

    mine = slot(row)

    def z_copy(up, step, q):
        block = row - (step - 1) if up else row + (step - 1)
        there = row + 1 if up else row - 1
        part = right.at[slot(block), pl.ds(q * per, per)]
        lane = 0 if up else 1
        return pltpu.make_async_remote_copy(
            src_ref=part,
            dst_ref=part,
            send_sem=z_send.at[lane, step - 1, q],
            recv_sem=z_recv.at[lane, step - 1, q],
            device_id={"row": there},
            device_id_type=MESH,
        )

    def z_land(up, step, q):
        block = row - step if up else row + step
        part = right.at[slot(block), pl.ds(q * per, per)]
        lane = 0 if up else 1
        return pltpu.make_async_remote_copy(
            src_ref=part,
            dst_ref=part,
            send_sem=z_send.at[lane, step - 1, q],
            recv_sem=z_recv.at[lane, step - 1, q],
            device_id={"row": row},
            device_id_type=MESH,
        )

    def sends(up, step):
        if up:
            return jnp.logical_and(row - (step - 1) >= 0, row + 1 < n_row)
        return jnp.logical_and(row + (step - 1) < n_row, row >= 1)

    def lands(up, step):
        return row - step >= 0 if up else row + step < n_row

    def start_send(step, q):
        for up in (True, False):

            @pl.when(sends(up, step))
            def _():
                z_copy(up, step, q).start()

    def wait_land(step, q):
        for up in (True, False):

            @pl.when(lands(up, step))
            def _():
                z_land(up, step, q).wait_recv()

    middle = jnp.where(row >= 1, 1, 0) + jnp.where(row + 1 < n_row, 1, 0)
    pl.semaphore_wait(barrier, middle + n_col)

    for q in range(CHUNKS):
        span = flat[pl.ds(q * per * rows, per * rows), :].astype(BF16)
        right[mine, pl.ds(q * per, per)] = span.reshape(per, rows, 128)
        start_send(1, q)

    for fetch in fetches[4:]:
        fetch.wait()
    wl[:slab] = turned(2, gain_in)
    wl[slab : 2 * slab] = turned(3, gain_in)
    wl[2 * slab :] = turned(4, gain_in)
    wo[...] = turned(5, gains[1])

    def left_step(t, carry):
        for u in range(STEP_GROUPS):
            g = t * STEP_GROUPS + u
            p = nt_dot(wl[...], zn[g])
            r = jax.nn.sigmoid(p[slab : 2 * slab]) * p[:slab]
            gate[g] = jax.nn.sigmoid(p[2 * slab :])
            first, second = interleave(r[:pairs], r[pairs:])
            flat[pl.ds(g, pairs, stride=rows), :] = first
            flat[pl.ds(g + half, pairs, stride=rows), :] = second
        return carry

    lax.fori_loop(0, half // STEP_GROUPS, left_step, 0)

    def left_mask(t, carry):
        for u in range(per):
            c = t * per + u
            f = flat[pl.ds(pl.multiple_of(c * rows, rows), rows), :]
            first = jnp.where(low, f, 0.0)
            second = jnp.where(low, 0.0, f)
            left[c] = jnp.concatenate(
                [first[:half], second[:half], first[half:], second[half:]], 0
            ).astype(BF16)
        return carry

    for step in range(1, n_row):
        for q in range(CHUNKS):
            if step == 1 and q == 0:
                lax.fori_loop(0, pairs // per, left_mask, 0)
            wait_land(step, q)
            if step + 1 < n_row:
                start_send(step + 1, q)
                continue
            contract(
                q, per, rows, n_row, n_col, col, left, right, keep, x_out, x_in,
                x_send, x_recv, interleave,
            )
            if q >= 1:
                combine(q - 1, per, n_col, col, chan, keep, x_out, x_in, tri, x_send, x_recv, s_send, s_recv)
    combine(CHUNKS - 1, per, n_col, col, chan, keep, x_out, x_in, tri, x_send, x_recv, s_send, s_recv)

    for q in range(CHUNKS):
        s_copy(1 - chan, q, per, chan, tri, s_send, s_recv).wait_recv()

    def stat_step(t, carry):
        total, square = carry
        for u in range(per):
            c = t * per + u
            for h in range(2):
                v = tri[h, c].astype(F32)
                a, b = v[:half], v[half:]
                total = total + (a + b)
                square = square + (a * a + b * b)
        return total, square

    zero = jnp.zeros((half, 128), F32)
    total, square = lax.fori_loop(0, pairs // per, stat_step, (zero, zero))
    mean = total * (1.0 / hidden)
    var = square * (1.0 / hidden) - mean * mean
    scale = lax.rsqrt(var + epsilon)

    def norm_step(t, carry):
        for u in range(per):
            c = t * per + u
            for h in range(2):
                v = tri[h, c].astype(F32)
                for k in range(2):
                    at = pl.multiple_of(((h * 2 + k) * pairs + c) * half, half)
                    flat_tri[pl.ds(at, half), :] = (v[k * half : (k + 1) * half] - mean) * scale
        return carry

    lax.fori_loop(0, pairs // per, norm_step, 0)

    def out_step(t, carry):
        for u in range(STEP_GROUPS):
            g = t * STEP_GROUPS + u
            v = flat_tri[pl.ds(g, hidden, stride=half), :].astype(BF16)
            y = jnp.dot(wo[...], v, preferred_element_type=F32) * gate[g]
            y = jnp.transpose(y).astype(BF16)
            out_ref[g] = y[:width]
            out_ref[g + half] = y[width:]
        return carry

    lax.fori_loop(0, half // STEP_GROUPS, out_step, 0)

    for step in range(1, n_row):
        for q in range(CHUNKS):
            for up in (True, False):

                @pl.when(sends(up, step))
                def _():
                    z_copy(up, step, q).wait_send()

    for q in range(CHUNKS):
        for d in range(1, n_col):
            x_copy(d, q, per, n_col, col, x_out, x_in, x_send, x_recv).wait_send()
        s_copy(chan, q, per, chan, tri, s_send, s_recv).wait_send()


def x_copy(d, q, per, n_col, col, x_out, x_in, x_send, x_recv):
    return pltpu.make_async_remote_copy(
        src_ref=x_out.at[d - 1, pl.ds(q * per, per)],
        dst_ref=x_in.at[d - 1, pl.ds(q * per, per)],
        send_sem=x_send.at[d - 1, q],
        recv_sem=x_recv.at[d - 1, q],
        device_id={"col": lax.rem(col + d, n_col)},
        device_id_type=MESH,
    )


def s_copy(which, q, per, chan, tri, s_send, s_recv):
    part = tri.at[which, pl.ds(q * per, per)]
    return pltpu.make_async_remote_copy(
        src_ref=part,
        dst_ref=part,
        send_sem=s_send.at[q],
        recv_sem=s_recv.at[q],
        device_id={"chan": 1 - chan},
        device_id_type=MESH,
    )


def contract(
    q, per, rows, n_row, n_col, col, left, right, keep, x_out, x_in, x_send, x_recv, interleave
):
    for u in range(per):
        c = q * per + u
        a = left[c]
        for m in range(n_col // 2):
            blocks = n_row // (n_col // 2)
            b = jnp.concatenate([right[m * blocks + s, c] for s in range(blocks)], 0)
            t = nt_dot(a, b)
            even, odd = interleave(t[:rows], t[rows:])
            if m == 0:
                keep[c] = even
            else:
                x_out[2 * m - 1, c] = even.astype(BF16)
            x_out[2 * m, c] = odd.astype(BF16)
    for d in range(1, n_col):
        x_copy(d, q, per, n_col, col, x_out, x_in, x_send, x_recv).start()


def combine(
    q, per, n_col, col, chan, keep, x_out, x_in, tri, x_send, x_recv, s_send, s_recv
):
    for d in range(1, n_col):
        x_copy(d, q, per, n_col, col, x_out, x_in, x_send, x_recv).wait_recv()
    for u in range(per):
        c = q * per + u
        v = keep[c]
        for d in range(1, n_col):
            v = v + x_in[d - 1, c].astype(F32)
        tri[chan, c] = v.astype(BF16)
    s_copy(chan, q, per, chan, tri, s_send, s_recv).start()


def on_device(pair_act, input_gain, lp, lg, rp, rg, output_gain, og, op):
    rows, width, channels = pair_act.shape
    hidden = lp.shape[1]
    slab = hidden // 2
    pairs = slab // 2
    half = rows // 2
    n_row = lax.axis_size("row")
    n_col = lax.axis_size("col")
    vmem = pl.BlockSpec(memory_space=pltpu.VMEM)
    dma = pltpu.SemaphoreType.DMA
    return pl.pallas_call(
        functools.partial(kernel, n_row, n_col),
        out_shape=jax.ShapeDtypeStruct((rows, width, channels // 2), BF16),
        in_specs=[pl.BlockSpec(memory_space=pltpu.HBM)] * 9,
        out_specs=vmem,
        scratch_shapes=[
            pltpu.VMEM((rows, width, channels), BF16),
            pltpu.VMEM((2, 1, 128), F32),
            pltpu.VMEM((6, channels, hidden), BF16),
            dma((9,)),
            pltpu.VMEM((2 * slab, channels), BF16),
            pltpu.VMEM((3 * slab, channels), BF16),
            pltpu.VMEM((channels // 2, hidden), BF16),
            pltpu.VMEM((half, 2 * width, channels), BF16),
            pltpu.VMEM((pairs * rows, 128), F32),
            pltpu.VMEM((half, channels // 2, 128), F32),
            pltpu.VMEM((pairs, 2 * rows, 128), BF16),
            pltpu.VMEM((n_row, pairs, rows, 128), BF16),
            pltpu.VMEM((pairs, rows, 128), F32),
            pltpu.VMEM((n_col - 1, pairs, rows, 128), BF16),
            pltpu.VMEM((n_col - 1, pairs, rows, 128), BF16),
            pltpu.VMEM((2, pairs, rows, 128), BF16),
            pltpu.VMEM((hidden * half, 128), F32),
            dma((2, n_row - 1, CHUNKS)),
            dma((2, n_row - 1, CHUNKS)),
            dma((n_col - 1, CHUNKS)),
            dma((n_col - 1, CHUNKS)),
            dma((CHUNKS,)),
            dma((CHUNKS,)),
        ],
        compiler_params=pltpu.CompilerParams(
            collective_id=0, has_side_effects=True, vmem_limit_bytes=60 * 2**20
        ),
    )(
        pair_act,
        input_gain.reshape(1, channels),
        lp,
        lg,
        rp,
        rg,
        output_gain.reshape(1, hidden),
        og,
        op,
    )


def solution(mesh):
    placed = (P(("crop", "row"), "col", None), P(), P(), P(), P(), P(), P(), P(), P())
    return jax.shard_map(
        on_device,
        mesh=mesh,
        in_specs=placed,
        out_specs=P(("crop", "row"), "col", "chan"),
        check_vma=False,
    )
```

```python
import functools

import jax
import jax.numpy as jnp
from jax import lax
from jax.experimental import pallas as pl
from jax.experimental.pallas import tpu as pltpu
from jax.sharding import PartitionSpec as P

epsilon = 1e-05
MESH = pl.DeviceIdType.MESH
F32 = jnp.float32
BF16 = jnp.bfloat16
CHUNKS = 4
STEP_GROUPS = 4


def nt_dot(a, b):
    return lax.dot_general(a, b, (((1,), (1,)), ((), ())), preferred_element_type=F32)


def kernel(
    n_row,
    n_col,
    pair_hbm,
    in_gain_hbm,
    lp_hbm,
    lg_hbm,
    rp_hbm,
    rg_hbm,
    out_gain_hbm,
    og_hbm,
    op_hbm,
    out_ref,
    pair_ref,
    gains,
    weights,
    in_sem,
    wr,
    wl,
    wo,
    zn,
    flat,
    gate,
    left,
    right,
    keep,
    x_out,
    x_in,
    tri,
    flat_tri,
    left_flat,
    left_end,
    far_out,
    far_in,
    z_send,
    z_recv,
    x_send,
    x_recv,
    s_send,
    s_recv,
):
    rows, width, channels = pair_hbm.shape
    half = rows // 2
    hidden = lp_hbm.shape[1]
    slab = hidden // 2
    pairs = slab // 2
    ratio = n_row // n_col
    per = pairs // CHUNKS
    row = lax.axis_index("row")
    col = lax.axis_index("col")
    chan = lax.axis_index("chan")

    def slot(block):
        return lax.rem(block - ratio * col + n_row, n_row)

    fetches = [
        pltpu.make_async_copy(source, target, in_sem.at[index])
        for index, (source, target) in enumerate(
            [
                (rp_hbm, weights.at[0]),
                (rg_hbm, weights.at[1]),
                (in_gain_hbm, gains.at[0]),
                (pair_hbm, pair_ref),
                (lp_hbm, weights.at[2]),
                (lg_hbm, weights.at[3]),
                (og_hbm, weights.at[4]),
                (op_hbm, weights.at[5]),
                (out_gain_hbm, gains.at[1]),
            ]
        )
    ]
    for fetch in fetches:
        fetch.start()

    barrier = pltpu.get_barrier_semaphore()

    @pl.when(row + 1 < n_row)
    def _():
        pl.semaphore_signal(barrier, inc=1, device_id={"row": row + 1}, device_id_type=MESH)

    @pl.when(row >= 1)
    def _():
        pl.semaphore_signal(barrier, inc=1, device_id={"row": row - 1}, device_id_type=MESH)

    for d in range(1, n_col):
        pl.semaphore_signal(
            barrier, inc=1, device_id={"col": lax.rem(col + d, n_col)}, device_id_type=MESH
        )
    pl.semaphore_signal(barrier, inc=1, device_id={"chan": 1 - chan}, device_id_type=MESH)

    def turned(index, gain):
        w = jnp.transpose(weights[index].astype(F32))
        w = jnp.where(chan == 0, w[:slab], w[slab:])
        return (w * gain).astype(BF16)

    for fetch in fetches[:3]:
        fetch.wait()
    gain_in = gains[0]
    wr[:slab] = turned(0, gain_in)
    wr[slab:] = turned(1, gain_in)
    fetches[3].wait()

    low = lax.broadcasted_iota(jnp.int32, (1, 128), 1) < width

    def interleave(a, b):
        first = jnp.where(low, a, pltpu.roll(b, width, 1))
        second = jnp.where(low, pltpu.roll(a, width, 1), b)
        return first, second

    def right_step(t, carry):
        for u in range(STEP_GROUPS):
            g = t * STEP_GROUPS + u
            x = jnp.concatenate([pair_ref[g], pair_ref[g + half]], 0).astype(F32)
            mean = jnp.mean(x, axis=-1, keepdims=True)
            var = jnp.mean(x * x, axis=-1, keepdims=True) - mean * mean
            z = ((x - mean) * lax.rsqrt(var + epsilon)).astype(BF16)
            zn[g] = z
            p = nt_dot(wr[...], z)
            r = jax.nn.sigmoid(p[slab:]) * p[:slab]
            first, second = interleave(r[:pairs], r[pairs:])
            flat[pl.ds(g, pairs, stride=rows), :] = first
            flat[pl.ds(g + half, pairs, stride=rows), :] = second
        return carry

    lax.fori_loop(0, half // STEP_GROUPS, right_step, 0)

    mine = slot(row)

    def z_copy(up, step, q):
        block = row - (step - 1) if up else row + (step - 1)
        there = row + 1 if up else row - 1
        part = right.at[slot(block), pl.ds(q * per, per)]
        lane = 0 if up else 1
        return pltpu.make_async_remote_copy(
            src_ref=part,
            dst_ref=part,
            send_sem=z_send.at[lane, step - 1, q],
            recv_sem=z_recv.at[lane, step - 1, q],
            device_id={"row": there},
            device_id_type=MESH,
        )

    def z_land(up, step, q):
        block = row - step if up else row + step
        part = right.at[slot(block), pl.ds(q * per, per)]
        lane = 0 if up else 1
        return pltpu.make_async_remote_copy(
            src_ref=part,
            dst_ref=part,
            send_sem=z_send.at[lane, step - 1, q],
            recv_sem=z_recv.at[lane, step - 1, q],
            device_id={"row": row},
            device_id_type=MESH,
        )

    def sends(up, step):
        if up:
            return jnp.logical_and(row - (step - 1) >= 0, row + 1 < n_row)
        return jnp.logical_and(row + (step - 1) < n_row, row >= 1)

    def lands(up, step):
        return row - step >= 0 if up else row + step < n_row

    def start_send(step, q):
        for up in (True, False):

            @pl.when(sends(up, step))
            def _():
                z_copy(up, step, q).start()

    def wait_land(step, q):
        for up in (True, False):

            @pl.when(lands(up, step))
            def _():
                z_land(up, step, q).wait_recv()

    line_of_four = n_row == 4 and n_col == 2
    helper = jnp.logical_or(row == 1, row == 2)
    end = jnp.logical_or(row == 0, row == 3)
    peer = row + 1 - 2 * lax.rem(row, 2)
    far_col = 1 - row // 2
    far_kept = far_col == col

    def hop(index, q, source, target, there):
        a, b = index
        return pltpu.make_async_remote_copy(
            src_ref=source.at[pl.ds(q * per, per)],
            dst_ref=target.at[pl.ds(q * per, per)],
            send_sem=z_send.at[a, b, q],
            recv_sem=z_recv.at[a, b, q],
            device_id={"row": there},
            device_id_type=MESH,
        )

    def block_hop(index, q, block, there):
        part = right.at[slot(block)]
        return hop(index, q, part, part, there)

    def to_peer(q):
        return block_hop((0, 0), q, row, peer)

    def from_peer(q):
        return block_hop((0, 0), q, peer, peer)

    def to_middle(q):
        return block_hop((0, 1), q, row, 3 - row)

    def from_middle(q):
        return block_hop((0, 1), q, 3 - row, 3 - row)

    def pass_on(q):
        return block_hop((0, 2), q, peer, 3 - row)

    def passed_on(q):
        return block_hop((0, 2), q, 3 - peer, 3 - row)

    def left_over(q):
        return hop((1, 0), q, left_flat, left_end, peer)

    def far_back(q):
        return hop((1, 1), q, far_out, far_in, peer)

    middle = jnp.where(row >= 1, 1, 0) + jnp.where(row + 1 < n_row, 1, 0)
    pl.semaphore_wait(barrier, middle + n_col)

    for q in range(CHUNKS):
        span = flat[pl.ds(q * per * rows, per * rows), :].astype(BF16)
        right[mine, pl.ds(q * per, per)] = span.reshape(per, rows, 128)
        if line_of_four:
            to_peer(q).start()

            @pl.when(helper)
            def _():
                to_middle(q).start()
        else:
            start_send(1, q)

    for fetch in fetches[4:]:
        fetch.wait()
    wl[:slab] = turned(2, gain_in)
    wl[slab : 2 * slab] = turned(3, gain_in)
    wl[2 * slab :] = turned(4, gain_in)
    wo[...] = turned(5, gains[1])

    def left_step(t, carry):
        for u in range(STEP_GROUPS):
            g = t * STEP_GROUPS + u
            p = nt_dot(wl[...], zn[g])
            r = jax.nn.sigmoid(p[slab : 2 * slab]) * p[:slab]
            gate[g] = jax.nn.sigmoid(p[2 * slab :])
            first, second = interleave(r[:pairs], r[pairs:])
            flat[pl.ds(g, pairs, stride=rows), :] = first
            flat[pl.ds(g + half, pairs, stride=rows), :] = second
        return carry

    lax.fori_loop(0, half // STEP_GROUPS, left_step, 0)

    def masked(f):
        first = jnp.where(low, f, 0.0)
        second = jnp.where(low, 0.0, f)
        return jnp.concatenate(
            [first[:half], second[:half], first[half:], second[half:]], 0
        ).astype(BF16)

    def left_mask(t, carry):
        for u in range(per):
            c = t * per + u
            f = flat[pl.ds(pl.multiple_of(c * rows, rows), rows), :]
            left[c] = masked(f)
            left_flat[c] = f.astype(BF16)
        return carry

    lax.fori_loop(0, pairs // per, left_mask, 0)

    for q in range(CHUNKS if line_of_four else 0):

        @pl.when(helper)
        def _():
            from_peer(q).wait_recv()
            pass_on(q).start()

        @pl.when(end)
        def _():
            to_peer(q).wait_send()
            left_over(q).start()
            from_peer(q).wait_recv()
            near = slot(2 * (row // 2))
            for u in range(per):
                c = q * per + u
                b = jnp.concatenate([right[near, c], right[near + 1, c]], 0)
                t = nt_dot(left[c], b)
                t = jnp.concatenate([t[:rows], t[rows:]], 1)
                keep[c] = t
                x_out[0, c] = t.astype(BF16)

            @pl.when(far_kept)
            def _():
                x_copy(1, q, per, n_col, col, x_out, x_in, x_send, x_recv).start()

    for q in range(CHUNKS if line_of_four else 0):

        @pl.when(helper)
        def _():
            from_middle(q).wait_recv()
            passed_on(q).wait_recv()
            left_over(q).wait_recv()
            for u in range(per):
                c = q * per + u
                a = masked(left_end[c].astype(F32))
                far = slot(2 * far_col)
                b = jnp.concatenate([right[far, c], right[far + 1, c]], 0)
                t = nt_dot(a, b)
                far_out[c] = jnp.concatenate([t[:rows], t[rows:]], 1).astype(BF16)
            far_back(q).start()
            contract(
                q, per, rows, n_row, n_col, col, left, right, keep, x_out, x_in,
                x_send, x_recv, interleave,
            )

        @pl.when(end)
        def _():
            far_back(q).wait_recv()

            @pl.when(far_kept)
            def _():
                for u in range(per):
                    c = q * per + u
                    keep[c] = far_in[c].astype(F32)

            @pl.when(jnp.logical_not(far_kept))
            def _():
                pltpu.make_async_remote_copy(
                    src_ref=far_in.at[pl.ds(q * per, per)],
                    dst_ref=x_in.at[0, pl.ds(q * per, per)],
                    send_sem=x_send.at[0, q],
                    recv_sem=x_recv.at[0, q],
                    device_id={"col": 1 - col},
                    device_id_type=MESH,
                ).start()

        if q >= 1:
            combine(q - 1, per, n_col, col, chan, keep, x_out, x_in, tri, x_send, x_recv, s_send, s_recv)

    for step in range(1, 1 if line_of_four else n_row):
        for q in range(CHUNKS):
            wait_land(step, q)
            if step + 1 < n_row:
                start_send(step + 1, q)
                continue
            contract(
                q, per, rows, n_row, n_col, col, left, right, keep, x_out, x_in,
                x_send, x_recv, interleave,
            )
            if q >= 1:
                combine(q - 1, per, n_col, col, chan, keep, x_out, x_in, tri, x_send, x_recv, s_send, s_recv)
    combine(CHUNKS - 1, per, n_col, col, chan, keep, x_out, x_in, tri, x_send, x_recv, s_send, s_recv)

    for q in range(CHUNKS):
        s_copy(1 - chan, q, per, chan, tri, s_send, s_recv).wait_recv()

    def stat_step(t, carry):
        total, square = carry
        for u in range(per):
            c = t * per + u
            for h in range(2):
                v = tri[h, c].astype(F32)
                a, b = v[:half], v[half:]
                total = total + (a + b)
                square = square + (a * a + b * b)
        return total, square

    zero = jnp.zeros((half, 128), F32)
    total, square = lax.fori_loop(0, pairs // per, stat_step, (zero, zero))
    mean = total * (1.0 / hidden)
    var = square * (1.0 / hidden) - mean * mean
    scale = lax.rsqrt(var + epsilon)

    def norm_step(t, carry):
        for u in range(per):
            c = t * per + u
            for h in range(2):
                v = tri[h, c].astype(F32)
                for k in range(2):
                    at = pl.multiple_of(((h * 2 + k) * pairs + c) * half, half)
                    flat_tri[pl.ds(at, half), :] = (v[k * half : (k + 1) * half] - mean) * scale
        return carry

    lax.fori_loop(0, pairs // per, norm_step, 0)

    def out_step(t, carry):
        for u in range(STEP_GROUPS):
            g = t * STEP_GROUPS + u
            v = flat_tri[pl.ds(g, hidden, stride=half), :].astype(BF16)
            y = jnp.dot(wo[...], v, preferred_element_type=F32) * gate[g]
            y = jnp.transpose(y).astype(BF16)
            out_ref[g] = y[:width]
            out_ref[g + half] = y[width:]
        return carry

    lax.fori_loop(0, half // STEP_GROUPS, out_step, 0)

    for q in range(CHUNKS if line_of_four else 0):

        @pl.when(helper)
        def _():
            to_peer(q).wait_send()
            to_middle(q).wait_send()
            pass_on(q).wait_send()
            far_back(q).wait_send()

        @pl.when(end)
        def _():
            left_over(q).wait_send()

    for step in range(1, 1 if line_of_four else n_row):
        for q in range(CHUNKS):
            for up in (True, False):

                @pl.when(sends(up, step))
                def _():
                    z_copy(up, step, q).wait_send()

    for q in range(CHUNKS):
        for d in range(1, n_col):
            x_copy(d, q, per, n_col, col, x_out, x_in, x_send, x_recv).wait_send()
        s_copy(chan, q, per, chan, tri, s_send, s_recv).wait_send()


def x_copy(d, q, per, n_col, col, x_out, x_in, x_send, x_recv):
    return pltpu.make_async_remote_copy(
        src_ref=x_out.at[d - 1, pl.ds(q * per, per)],
        dst_ref=x_in.at[d - 1, pl.ds(q * per, per)],
        send_sem=x_send.at[d - 1, q],
        recv_sem=x_recv.at[d - 1, q],
        device_id={"col": lax.rem(col + d, n_col)},
        device_id_type=MESH,
    )


def s_copy(which, q, per, chan, tri, s_send, s_recv):
    part = tri.at[which, pl.ds(q * per, per)]
    return pltpu.make_async_remote_copy(
        src_ref=part,
        dst_ref=part,
        send_sem=s_send.at[q],
        recv_sem=s_recv.at[q],
        device_id={"chan": 1 - chan},
        device_id_type=MESH,
    )


def contract(
    q, per, rows, n_row, n_col, col, left, right, keep, x_out, x_in, x_send, x_recv, interleave
):
    for u in range(per):
        c = q * per + u
        a = left[c]
        for m in range(n_col // 2):
            blocks = n_row // (n_col // 2)
            b = jnp.concatenate([right[m * blocks + s, c] for s in range(blocks)], 0)
            t = nt_dot(a, b)
            even, odd = interleave(t[:rows], t[rows:])
            if m == 0:
                keep[c] = even
            else:
                x_out[2 * m - 1, c] = even.astype(BF16)
            x_out[2 * m, c] = odd.astype(BF16)
    for d in range(1, n_col):
        x_copy(d, q, per, n_col, col, x_out, x_in, x_send, x_recv).start()


def combine(
    q, per, n_col, col, chan, keep, x_out, x_in, tri, x_send, x_recv, s_send, s_recv
):
    for d in range(1, n_col):
        x_copy(d, q, per, n_col, col, x_out, x_in, x_send, x_recv).wait_recv()
    for u in range(per):
        c = q * per + u
        v = keep[c]
        for d in range(1, n_col):
            v = v + x_in[d - 1, c].astype(F32)
        tri[chan, c] = v.astype(BF16)
    s_copy(chan, q, per, chan, tri, s_send, s_recv).start()


def on_device(pair_act, input_gain, lp, lg, rp, rg, output_gain, og, op):
    rows, width, channels = pair_act.shape
    hidden = lp.shape[1]
    slab = hidden // 2
    pairs = slab // 2
    half = rows // 2
    n_row = lax.axis_size("row")
    n_col = lax.axis_size("col")
    vmem = pl.BlockSpec(memory_space=pltpu.VMEM)
    dma = pltpu.SemaphoreType.DMA
    return pl.pallas_call(
        functools.partial(kernel, n_row, n_col),
        out_shape=jax.ShapeDtypeStruct((rows, width, channels // 2), BF16),
        in_specs=[pl.BlockSpec(memory_space=pltpu.HBM)] * 9,
        out_specs=vmem,
        scratch_shapes=[
            pltpu.VMEM((rows, width, channels), BF16),
            pltpu.VMEM((2, 1, 128), F32),
            pltpu.VMEM((6, channels, hidden), BF16),
            dma((9,)),
            pltpu.VMEM((2 * slab, channels), BF16),
            pltpu.VMEM((3 * slab, channels), BF16),
            pltpu.VMEM((channels // 2, hidden), BF16),
            pltpu.VMEM((half, 2 * width, channels), BF16),
            pltpu.VMEM((pairs * rows, 128), F32),
            pltpu.VMEM((half, channels // 2, 128), F32),
            pltpu.VMEM((pairs, 2 * rows, 128), BF16),
            pltpu.VMEM((n_row, pairs, rows, 128), BF16),
            pltpu.VMEM((pairs, rows, 128), F32),
            pltpu.VMEM((n_col - 1, pairs, rows, 128), BF16),
            pltpu.VMEM((n_col - 1, pairs, rows, 128), BF16),
            pltpu.VMEM((2, pairs, rows, 128), BF16),
            pltpu.VMEM((hidden * half, 128), F32),
            pltpu.VMEM((pairs, rows, 128), BF16),
            pltpu.VMEM((pairs, rows, 128), BF16),
            pltpu.VMEM((pairs, rows, 128), BF16),
            pltpu.VMEM((pairs, rows, 128), BF16),
            dma((2, n_row - 1, CHUNKS)),
            dma((2, n_row - 1, CHUNKS)),
            dma((n_col - 1, CHUNKS)),
            dma((n_col - 1, CHUNKS)),
            dma((CHUNKS,)),
            dma((CHUNKS,)),
        ],
        compiler_params=pltpu.CompilerParams(
            collective_id=0, has_side_effects=True, vmem_limit_bytes=60 * 2**20
        ),
    )(
        pair_act,
        input_gain.reshape(1, channels),
        lp,
        lg,
        rp,
        rg,
        output_gain.reshape(1, hidden),
        og,
        op,
    )


def solution(mesh):
    placed = (P(("crop", "row"), "col", None), P(), P(), P(), P(), P(), P(), P(), P())
    return jax.shard_map(
        on_device,
        mesh=mesh,
        in_specs=placed,
        out_specs=P(("crop", "row"), "col", "chan"),
        check_vma=False,
    )
```

```python
import functools

import jax
import jax.numpy as jnp
from jax import lax
from jax.experimental import pallas as pl
from jax.experimental.pallas import tpu as pltpu
from jax.sharding import PartitionSpec as P

epsilon = 1e-05
MESH = pl.DeviceIdType.MESH
F32 = jnp.float32
BF16 = jnp.bfloat16
CHUNKS = 4
STEP_GROUPS = 8


def nt_dot(a, b):
    return lax.dot_general(a, b, (((1,), (1,)), ((), ())), preferred_element_type=F32)


def kernel(
    n_row,
    n_col,
    pair_hbm,
    in_gain_hbm,
    lp_hbm,
    lg_hbm,
    rp_hbm,
    rg_hbm,
    out_gain_hbm,
    og_hbm,
    op_hbm,
    out_ref,
    pair_ref,
    gains,
    weights,
    in_sem,
    wr,
    wl,
    wo,
    zn,
    flat,
    gate,
    left,
    right,
    keep,
    x_out,
    x_in,
    tri,
    flat_tri,
    left_flat,
    left_end,
    far_out,
    far_in,
    z_send,
    z_recv,
    x_send,
    x_recv,
    s_send,
    s_recv,
):
    rows, width, channels = pair_hbm.shape
    half = rows // 2
    hidden = lp_hbm.shape[1]
    slab = hidden // 2
    pairs = slab // 2
    ratio = n_row // n_col
    per = pairs // CHUNKS
    row = lax.axis_index("row")
    col = lax.axis_index("col")
    chan = lax.axis_index("chan")

    def slot(block):
        return lax.rem(block - ratio * col + n_row, n_row)

    fetches = [
        pltpu.make_async_copy(source, target, in_sem.at[index])
        for index, (source, target) in enumerate(
            [
                (rp_hbm, weights.at[0]),
                (rg_hbm, weights.at[1]),
                (in_gain_hbm, gains.at[0]),
                (pair_hbm, pair_ref),
                (lp_hbm, weights.at[2]),
                (lg_hbm, weights.at[3]),
                (og_hbm, weights.at[4]),
                (op_hbm, weights.at[5]),
                (out_gain_hbm, gains.at[1]),
            ]
        )
    ]
    for fetch in fetches:
        fetch.start()

    barrier = pltpu.get_barrier_semaphore()

    @pl.when(row + 1 < n_row)
    def _():
        pl.semaphore_signal(barrier, inc=1, device_id={"row": row + 1}, device_id_type=MESH)

    @pl.when(row >= 1)
    def _():
        pl.semaphore_signal(barrier, inc=1, device_id={"row": row - 1}, device_id_type=MESH)

    for d in range(1, n_col):
        pl.semaphore_signal(
            barrier, inc=1, device_id={"col": lax.rem(col + d, n_col)}, device_id_type=MESH
        )
    pl.semaphore_signal(barrier, inc=1, device_id={"chan": 1 - chan}, device_id_type=MESH)

    def turned(index, gain):
        w = jnp.transpose(weights[index].astype(F32))
        w = jnp.where(chan == 0, w[:slab], w[slab:])
        return (w * gain).astype(BF16)

    for fetch in fetches[:3]:
        fetch.wait()
    gain_in = gains[0]
    wr[:slab] = turned(0, gain_in)
    wr[slab:] = turned(1, gain_in)
    fetches[3].wait()

    low = lax.broadcasted_iota(jnp.int32, (1, 128), 1) < width

    def interleave(a, b):
        first = jnp.where(low, a, pltpu.roll(b, width, 1))
        second = jnp.where(low, pltpu.roll(a, width, 1), b)
        return first, second

    def right_step(t, carry):
        for u in range(STEP_GROUPS):
            g = t * STEP_GROUPS + u
            x = jnp.concatenate([pair_ref[g], pair_ref[g + half]], 0).astype(F32)
            mean = jnp.mean(x, axis=-1, keepdims=True)
            var = jnp.mean(x * x, axis=-1, keepdims=True) - mean * mean
            z = ((x - mean) * lax.rsqrt(var + epsilon)).astype(BF16)
            zn[g] = z
            p = nt_dot(wr[...], z)
            r = jax.nn.sigmoid(p[slab:]) * p[:slab]
            first, second = interleave(r[:pairs], r[pairs:])
            flat[pl.ds(g, pairs, stride=rows), :] = first
            flat[pl.ds(g + half, pairs, stride=rows), :] = second
        return carry

    lax.fori_loop(0, half // STEP_GROUPS, right_step, 0)

    mine = slot(row)

    def z_copy(up, step, q):
        block = row - (step - 1) if up else row + (step - 1)
        there = row + 1 if up else row - 1
        part = right.at[slot(block), pl.ds(q * per, per)]
        lane = 0 if up else 1
        return pltpu.make_async_remote_copy(
            src_ref=part,
            dst_ref=part,
            send_sem=z_send.at[lane, step - 1, q],
            recv_sem=z_recv.at[lane, step - 1, q],
            device_id={"row": there},
            device_id_type=MESH,
        )

    def z_land(up, step, q):
        block = row - step if up else row + step
        part = right.at[slot(block), pl.ds(q * per, per)]
        lane = 0 if up else 1
        return pltpu.make_async_remote_copy(
            src_ref=part,
            dst_ref=part,
            send_sem=z_send.at[lane, step - 1, q],
            recv_sem=z_recv.at[lane, step - 1, q],
            device_id={"row": row},
            device_id_type=MESH,
        )

    def sends(up, step):
        if up:
            return jnp.logical_and(row - (step - 1) >= 0, row + 1 < n_row)
        return jnp.logical_and(row + (step - 1) < n_row, row >= 1)

    def lands(up, step):
        return row - step >= 0 if up else row + step < n_row

    def start_send(step, q):
        for up in (True, False):

            @pl.when(sends(up, step))
            def _():
                z_copy(up, step, q).start()

    def wait_land(step, q):
        for up in (True, False):

            @pl.when(lands(up, step))
            def _():
                z_land(up, step, q).wait_recv()

    line_of_four = n_row == 4 and n_col == 2
    helper = jnp.logical_or(row == 1, row == 2)
    end = jnp.logical_or(row == 0, row == 3)
    peer = row + 1 - 2 * lax.rem(row, 2)
    far_col = 1 - row // 2
    far_kept = far_col == col

    def hop(index, q, source, target, there):
        a, b = index
        return pltpu.make_async_remote_copy(
            src_ref=source.at[pl.ds(q * per, per)],
            dst_ref=target.at[pl.ds(q * per, per)],
            send_sem=z_send.at[a, b, q],
            recv_sem=z_recv.at[a, b, q],
            device_id={"row": there},
            device_id_type=MESH,
        )

    def block_hop(index, q, block, there):
        part = right.at[slot(block)]
        return hop(index, q, part, part, there)

    def to_peer(q):
        return block_hop((0, 0), q, row, peer)

    def from_peer(q):
        return block_hop((0, 0), q, peer, peer)

    def to_middle(q):
        return block_hop((0, 1), q, row, 3 - row)

    def from_middle(q):
        return block_hop((0, 1), q, 3 - row, 3 - row)

    def pass_on(q):
        return block_hop((0, 2), q, peer, 3 - row)

    def passed_on(q):
        return block_hop((0, 2), q, 3 - peer, 3 - row)

    def left_over(q):
        return hop((1, 0), q, left_flat, left_end, peer)

    def far_back(q):
        return hop((1, 1), q, far_out, far_in, peer)

    middle = jnp.where(row >= 1, 1, 0) + jnp.where(row + 1 < n_row, 1, 0)
    pl.semaphore_wait(barrier, middle + n_col)

    for q in range(CHUNKS):
        span = flat[pl.ds(q * per * rows, per * rows), :].astype(BF16)
        right[mine, pl.ds(q * per, per)] = span.reshape(per, rows, 128)
        if line_of_four:
            to_peer(q).start()

            @pl.when(helper)
            def _():
                to_middle(q).start()
        else:
            start_send(1, q)

    for fetch in fetches[4:]:
        fetch.wait()
    wl[:slab] = turned(2, gain_in)
    wl[slab : 2 * slab] = turned(3, gain_in)
    wl[2 * slab :] = turned(4, gain_in)
    wo[...] = turned(5, gains[1])

    def left_step(t, carry):
        for u in range(STEP_GROUPS):
            g = t * STEP_GROUPS + u
            p = nt_dot(wl[...], zn[g])
            r = jax.nn.sigmoid(p[slab : 2 * slab]) * p[:slab]
            gate[g] = jax.nn.sigmoid(p[2 * slab :])
            first, second = interleave(r[:pairs], r[pairs:])
            flat[pl.ds(g, pairs, stride=rows), :] = first
            flat[pl.ds(g + half, pairs, stride=rows), :] = second
        return carry

    lax.fori_loop(0, half // STEP_GROUPS, left_step, 0)

    def masked(f):
        first = jnp.where(low, f, 0.0)
        second = jnp.where(low, 0.0, f)
        return jnp.concatenate(
            [first[:half], second[:half], first[half:], second[half:]], 0
        ).astype(BF16)

    def left_mask(t, carry):
        for u in range(per):
            c = t * per + u
            f = flat[pl.ds(pl.multiple_of(c * rows, rows), rows), :]
            left[c] = masked(f)
            left_flat[c] = f.astype(BF16)
        return carry

    lax.fori_loop(0, pairs // per, left_mask, 0)

    for q in range(CHUNKS if line_of_four else 0):

        @pl.when(helper)
        def _():
            from_peer(q).wait_recv()
            pass_on(q).start()

        @pl.when(end)
        def _():
            to_peer(q).wait_send()
            left_over(q).start()
            from_peer(q).wait_recv()
            near = slot(2 * (row // 2))
            for u in range(per):
                c = q * per + u
                b = jnp.concatenate([right[near, c], right[near + 1, c]], 0)
                t = nt_dot(left[c], b)
                t = jnp.concatenate([t[:rows], t[rows:]], 1)
                keep[c] = t
                x_out[0, c] = t.astype(BF16)

            @pl.when(far_kept)
            def _():
                x_copy(1, q, per, n_col, col, x_out, x_in, x_send, x_recv).start()

    for q in range(CHUNKS if line_of_four else 0):

        @pl.when(helper)
        def _():
            from_middle(q).wait_recv()
            passed_on(q).wait_recv()
            left_over(q).wait_recv()
            for u in range(per):
                c = q * per + u
                a = masked(left_end[c].astype(F32))
                far = slot(2 * far_col)
                b = jnp.concatenate([right[far, c], right[far + 1, c]], 0)
                t = nt_dot(a, b)
                far_out[c] = jnp.concatenate([t[:rows], t[rows:]], 1).astype(BF16)
            far_back(q).start()
            contract(
                q, per, rows, n_row, n_col, col, left, right, keep, x_out, x_in,
                x_send, x_recv, interleave,
            )

        @pl.when(end)
        def _():
            far_back(q).wait_recv()

            @pl.when(far_kept)
            def _():
                for u in range(per):
                    c = q * per + u
                    keep[c] = far_in[c].astype(F32)

            @pl.when(jnp.logical_not(far_kept))
            def _():
                pltpu.make_async_remote_copy(
                    src_ref=far_in.at[pl.ds(q * per, per)],
                    dst_ref=x_in.at[0, pl.ds(q * per, per)],
                    send_sem=x_send.at[0, q],
                    recv_sem=x_recv.at[0, q],
                    device_id={"col": 1 - col},
                    device_id_type=MESH,
                ).start()


    for step in range(1, 1 if line_of_four else n_row):
        for q in range(CHUNKS):
            wait_land(step, q)
            if step + 1 < n_row:
                start_send(step + 1, q)
                continue
            contract(
                q, per, rows, n_row, n_col, col, left, right, keep, x_out, x_in,
                x_send, x_recv, interleave,
            )
            if q >= 1:
                combine(q - 1, per, n_col, col, chan, keep, x_out, x_in, tri, x_send, x_recv, s_send, s_recv)
    for q in range(0 if line_of_four else CHUNKS - 1, CHUNKS):
        combine(q, per, n_col, col, chan, keep, x_out, x_in, tri, x_send, x_recv, s_send, s_recv)

    for q in range(CHUNKS):
        s_copy(1 - chan, q, per, chan, tri, s_send, s_recv).wait_recv()

    def stat_step(t, carry):
        total, square = carry
        for u in range(per):
            c = t * per + u
            for h in range(2):
                v = tri[h, c].astype(F32)
                a, b = v[:half], v[half:]
                total = total + (a + b)
                square = square + (a * a + b * b)
        return total, square

    zero = jnp.zeros((half, 128), F32)
    total, square = lax.fori_loop(0, pairs // per, stat_step, (zero, zero))
    mean = total * (1.0 / hidden)
    var = square * (1.0 / hidden) - mean * mean
    scale = lax.rsqrt(var + epsilon)

    def norm_step(t, carry):
        for u in range(per):
            c = t * per + u
            for h in range(2):
                v = tri[h, c].astype(F32)
                for k in range(2):
                    at = pl.multiple_of(((h * 2 + k) * pairs + c) * half, half)
                    flat_tri[pl.ds(at, half), :] = (v[k * half : (k + 1) * half] - mean) * scale
        return carry

    lax.fori_loop(0, pairs // per, norm_step, 0)

    def out_step(t, carry):
        for u in range(STEP_GROUPS):
            g = t * STEP_GROUPS + u
            v = flat_tri[pl.ds(g, hidden, stride=half), :].astype(BF16)
            y = jnp.dot(wo[...], v, preferred_element_type=F32) * gate[g]
            y = jnp.transpose(y).astype(BF16)
            out_ref[g] = y[:width]
            out_ref[g + half] = y[width:]
        return carry

    lax.fori_loop(0, half // STEP_GROUPS, out_step, 0)

    for q in range(CHUNKS if line_of_four else 0):

        @pl.when(helper)
        def _():
            to_peer(q).wait_send()
            to_middle(q).wait_send()
            pass_on(q).wait_send()
            far_back(q).wait_send()

        @pl.when(end)
        def _():
            left_over(q).wait_send()

    for step in range(1, 1 if line_of_four else n_row):
        for q in range(CHUNKS):
            for up in (True, False):

                @pl.when(sends(up, step))
                def _():
                    z_copy(up, step, q).wait_send()

    for q in range(CHUNKS):
        for d in range(1, n_col):
            x_copy(d, q, per, n_col, col, x_out, x_in, x_send, x_recv).wait_send()
        s_copy(chan, q, per, chan, tri, s_send, s_recv).wait_send()


def x_copy(d, q, per, n_col, col, x_out, x_in, x_send, x_recv):
    return pltpu.make_async_remote_copy(
        src_ref=x_out.at[d - 1, pl.ds(q * per, per)],
        dst_ref=x_in.at[d - 1, pl.ds(q * per, per)],
        send_sem=x_send.at[d - 1, q],
        recv_sem=x_recv.at[d - 1, q],
        device_id={"col": lax.rem(col + d, n_col)},
        device_id_type=MESH,
    )


def s_copy(which, q, per, chan, tri, s_send, s_recv):
    part = tri.at[which, pl.ds(q * per, per)]
    return pltpu.make_async_remote_copy(
        src_ref=part,
        dst_ref=part,
        send_sem=s_send.at[q],
        recv_sem=s_recv.at[q],
        device_id={"chan": 1 - chan},
        device_id_type=MESH,
    )


def contract(
    q, per, rows, n_row, n_col, col, left, right, keep, x_out, x_in, x_send, x_recv, interleave
):
    for u in range(per):
        c = q * per + u
        a = left[c]
        for m in range(n_col // 2):
            blocks = n_row // (n_col // 2)
            b = jnp.concatenate([right[m * blocks + s, c] for s in range(blocks)], 0)
            t = nt_dot(a, b)
            even, odd = interleave(t[:rows], t[rows:])
            if m == 0:
                keep[c] = even
            else:
                x_out[2 * m - 1, c] = even.astype(BF16)
            x_out[2 * m, c] = odd.astype(BF16)
    for d in range(1, n_col):
        x_copy(d, q, per, n_col, col, x_out, x_in, x_send, x_recv).start()


def combine(
    q, per, n_col, col, chan, keep, x_out, x_in, tri, x_send, x_recv, s_send, s_recv
):
    for d in range(1, n_col):
        x_copy(d, q, per, n_col, col, x_out, x_in, x_send, x_recv).wait_recv()
    for u in range(per):
        c = q * per + u
        v = keep[c]
        for d in range(1, n_col):
            v = v + x_in[d - 1, c].astype(F32)
        tri[chan, c] = v.astype(BF16)
    s_copy(chan, q, per, chan, tri, s_send, s_recv).start()


def on_device(pair_act, input_gain, lp, lg, rp, rg, output_gain, og, op):
    rows, width, channels = pair_act.shape
    hidden = lp.shape[1]
    slab = hidden // 2
    pairs = slab // 2
    half = rows // 2
    n_row = lax.axis_size("row")
    n_col = lax.axis_size("col")
    vmem = pl.BlockSpec(memory_space=pltpu.VMEM)
    dma = pltpu.SemaphoreType.DMA
    return pl.pallas_call(
        functools.partial(kernel, n_row, n_col),
        out_shape=jax.ShapeDtypeStruct((rows, width, channels // 2), BF16),
        in_specs=[pl.BlockSpec(memory_space=pltpu.HBM)] * 9,
        out_specs=vmem,
        scratch_shapes=[
            pltpu.VMEM((rows, width, channels), BF16),
            pltpu.VMEM((2, 1, 128), F32),
            pltpu.VMEM((6, channels, hidden), BF16),
            dma((9,)),
            pltpu.VMEM((2 * slab, channels), BF16),
            pltpu.VMEM((3 * slab, channels), BF16),
            pltpu.VMEM((channels // 2, hidden), BF16),
            pltpu.VMEM((half, 2 * width, channels), BF16),
            pltpu.VMEM((pairs * rows, 128), F32),
            pltpu.VMEM((half, channels // 2, 128), F32),
            pltpu.VMEM((pairs, 2 * rows, 128), BF16),
            pltpu.VMEM((n_row, pairs, rows, 128), BF16),
            pltpu.VMEM((pairs, rows, 128), F32),
            pltpu.VMEM((n_col - 1, pairs, rows, 128), BF16),
            pltpu.VMEM((n_col - 1, pairs, rows, 128), BF16),
            pltpu.VMEM((2, pairs, rows, 128), BF16),
            pltpu.VMEM((hidden * half, 128), F32),
            pltpu.VMEM((pairs, rows, 128), BF16),
            pltpu.VMEM((pairs, rows, 128), BF16),
            pltpu.VMEM((pairs, rows, 128), BF16),
            pltpu.VMEM((pairs, rows, 128), BF16),
            dma((2, n_row - 1, CHUNKS)),
            dma((2, n_row - 1, CHUNKS)),
            dma((n_col - 1, CHUNKS)),
            dma((n_col - 1, CHUNKS)),
            dma((CHUNKS,)),
            dma((CHUNKS,)),
        ],
        compiler_params=pltpu.CompilerParams(
            collective_id=0, has_side_effects=True, vmem_limit_bytes=60 * 2**20
        ),
    )(
        pair_act,
        input_gain.reshape(1, channels),
        lp,
        lg,
        rp,
        rg,
        output_gain.reshape(1, hidden),
        og,
        op,
    )


def solution(mesh):
    placed = (P(("crop", "row"), "col", None), P(), P(), P(), P(), P(), P(), P(), P())
    return jax.shard_map(
        on_device,
        mesh=mesh,
        in_specs=placed,
        out_specs=P(("crop", "row"), "col", "chan"),
        check_vma=False,
    )
```
